32 devices in a mesh: groups: 2 (over x), ctx: 8 (over z, y), dp: 2 (over core).
Axes of the slice: x: 2, y: 2, z: 4, core: 2. Of those that a mesh axis runs over, the one named last changes fastest.
Arguments:
- inputs: bfloat16 [4, 4096, 256], P(('groups', 'dp'), 'ctx'), parts along dimension 0, may hold values from -6 to 6
- value_weight: bfloat16 [256, 256], replicated, may hold values from -0.375 to 0.375
- gate_weight: bfloat16 [256, 256], replicated, may hold values from -0.375 to 0.375
- output_weight: bfloat16 [256, 256], replicated, may hold values from -0.375 to 0.375
- filters: bfloat16 [4096, 256], P('ctx'), may hold values from -0.09375 to 0.09375
- cotangent: bfloat16 [4, 4096, 256], P(('groups', 'dp'), 'ctx'), parts along dimension 0, may hold values from -6 to 6
Outputs:
- input_grad: bfloat16 [4, 4096, 256], P(('groups', 'dp'), 'ctx'), parts along dimension 0
- proj_grads: float32 [6, 256, 256], P('groups', 'ctx'), parts along dimension 0
- filter_grads: float32 [8192, 256], P(('groups', 'ctx')), parts along dimension 0
The draws below stay inside these ranges and needn't reach their ends.
There are 2 independent parts, one for each index of `groups`. The reference program is written for one: setup_inputs(seed, part) draws one part's arguments, and reference() takes and returns one part's arrays. A program takes and returns all parts, laid end to end along the dimension named above; an argument that names none is the same for every part. Nothing has to cross between parts.
All inputs are finite; a program needn't handle non-finite values.
Results may differ from the reference program's by a relative error of at most 0.0057.
Values may be sent and summed in bfloat16 or wider, within the bound.
A program may use at most 64 MiB of HBM per device.

```python
import math
import jax
import jax.numpy as jnp

D = 256
SEQS = 2
LENGTH = 4096
TAPS = 4096


def shard_levels(stream_key, extent, shards, least, high):
    level = 1.0
    for dim, parts in shards:
        heights = jax.random.uniform(jax.random.fold_in(jax.random.fold_in(stream_key, 6), dim), (parts,), jnp.float32, least / len(shards), high / len(shards))
        level = level * jnp.repeat(jnp.exp(heights), extent[dim] // parts).reshape((-1,) + (1,) * (len(extent) - 1 - dim))
    return level


def normal_values(stream_key, shape, width, limit, cuts=(), held_as=jnp.bfloat16):
    level = shard_levels(stream_key, shape, cuts, -0.22, 0.18) if cuts else 1.0
    values = jax.random.normal(stream_key, shape, jnp.float32) * width * level
    return jnp.minimum(jnp.maximum(values, -limit), limit).astype(held_as)


def setup_inputs(seed: int = 0, part: int = 0) -> dict:
    key_list = jax.random.split(jax.random.key(seed), 7)
    part_keys = jax.random.split(jax.random.fold_in(key_list[6], part), 7)
    return {
        "inputs": normal_values(part_keys[0], (SEQS, LENGTH, D), 1.0, 6.0, ((0, 2), (1, 8))),
        "value_weight": normal_values(key_list[1], (D, D), D ** -0.5, 0.375),
        "gate_weight": normal_values(key_list[2], (D, D), D ** -0.5, 0.375),
        "output_weight": normal_values(key_list[3], (D, D), D ** -0.5, 0.375),
        "filters": normal_values(key_list[4], (TAPS, D), TAPS ** -0.5, 0.09375, ((0, 8),)),
        "cotangent": normal_values(part_keys[5], (SEQS, LENGTH, D), 1.0, 6.0, ((0, 2), (1, 8))),
    }


def reference(inputs, value_weight, gate_weight, output_weight, filters, cotangent):
    kernel_freq = jnp.fft.rfft(filters.astype(jnp.float32), axis=0)
    grad_scale = 1.0 / math.sqrt(SEQS * LENGTH)
    value_sum = jnp.zeros((D, D), jnp.float32)
    gate_sum = jnp.zeros((D, D), jnp.float32)
    output_sum = jnp.zeros((D, D), jnp.float32)
    kernel_sum = jnp.zeros((LENGTH, D), jnp.float32)
    grads_out = []
    for seq_index in range(SEQS):
        token_rows = inputs[seq_index]
        upstream = cotangent[seq_index]
        value_act = jnp.dot(token_rows, value_weight, preferred_element_type=jnp.float32).astype(jnp.bfloat16)
        gate_act = jnp.dot(token_rows, gate_weight, preferred_element_type=jnp.float32)
        value_freq = jnp.fft.rfft(value_act.astype(jnp.float32), axis=0)
        mixed_act = jnp.fft.irfft(value_freq * kernel_freq, n=LENGTH, axis=0).astype(jnp.float32)
        d_gated = jnp.dot(upstream, output_weight.T, preferred_element_type=jnp.float32)
        d_mixed = (d_gated * gate_act).astype(jnp.bfloat16)
        grad_freq = jnp.fft.rfft(d_mixed.astype(jnp.float32), axis=0)
        d_value = jnp.fft.irfft(grad_freq * jnp.conj(kernel_freq), n=LENGTH, axis=0).astype(jnp.bfloat16)
        correlation = jnp.fft.irfft(grad_freq * jnp.conj(value_freq), n=LENGTH, axis=0).astype(jnp.float32)
        gated = (gate_act * mixed_act).astype(jnp.bfloat16)
        d_gate = (d_gated * mixed_act).astype(jnp.bfloat16)
        input_rows = jnp.dot(d_value, value_weight.T, preferred_element_type=jnp.float32)
        input_rows = input_rows + jnp.dot(d_gate, gate_weight.T, preferred_element_type=jnp.float32)
        grads_out.append(input_rows.astype(jnp.bfloat16))
        value_sum = value_sum + jnp.dot(token_rows.T, d_value, preferred_element_type=jnp.float32)
        gate_sum = gate_sum + jnp.dot(token_rows.T, d_gate, preferred_element_type=jnp.float32)
        output_sum = output_sum + jnp.dot(gated.T, upstream, preferred_element_type=jnp.float32)
        kernel_sum = kernel_sum + correlation
    input_grad = jnp.stack(grads_out, axis=0)
    proj_grads = jnp.stack([value_sum, gate_sum, output_sum], axis=0) * grad_scale
    filter_grads = kernel_sum * grad_scale
    return (input_grad, proj_grads, filter_grads)
```

```python
import functools
import math

import jax
import jax.numpy as jnp
import numpy as np
from jax import lax
from jax.experimental import pallas as pl
from jax.experimental.pallas import tpu as pltpu
from jax.sharding import PartitionSpec as P

LANES = 128
AXES = ("ctx", "dp")


def dft_tables(length):
    outer = length // LANES
    k_outer = np.arange(outer)
    k_inner = np.arange(LANES)
    first = 2.0 * np.pi / outer * (np.outer(k_outer, k_outer) % outer)
    turn = 2.0 * np.pi / length * (np.outer(k_outer, k_inner) % length)
    second = 2.0 * np.pi / LANES * (np.outer(k_inner, k_inner) % LANES)
    cos_first, sin_first = np.cos(first), np.sin(first)
    cos_second, sin_second = np.cos(second), np.sin(second)
    forward_first = np.concatenate([cos_first, -sin_first], axis=0)
    inverse_first = np.concatenate([cos_first, -sin_first], axis=1) / length
    forward_second = np.block([[cos_second, -sin_second], [sin_second, cos_second]])
    inverse_second = np.block([[cos_second, sin_second], [-sin_second, cos_second]])
    as_float = [
        table.astype(np.float32)
        for table in (forward_first, inverse_first, forward_second, inverse_second)
    ]
    cos_turn = np.cos(turn).astype(np.float32)[:, None, :]
    sin_turn = np.sin(turn).astype(np.float32)[:, None, :]
    return as_float + [cos_turn, sin_turn]


def split(value):
    high = value.astype(jnp.bfloat16)
    low = (value - high.astype(jnp.float32)).astype(jnp.bfloat16)
    return high, low


def split_table(table):
    high = table.astype(jnp.bfloat16)
    return high, (table - high.astype(np.float32)).astype(jnp.bfloat16)


def dot(left, right):
    return jnp.dot(left, right, preferred_element_type=jnp.float32)


def contract(left, left_dim, right, right_dim):
    return lax.dot_general(
        left, right, (((left_dim,), (right_dim,)), ((), ())), preferred_element_type=jnp.float32
    )


def exchange_kernel(count, seqs, sent, held, send_sem, recv_sem, own_sem):
    peers = count * seqs
    me = lax.axis_index("ctx") * seqs + lax.axis_index("dp")
    barrier = pltpu.get_barrier_semaphore()

    def place(step):
        peer = lax.rem(me + step, peers)
        return peer, {"ctx": lax.div(peer, seqs), "dp": lax.rem(peer, seqs)}

    def greet(step, carry):
        pl.semaphore_signal(
            barrier, inc=1, device_id=place(step)[1], device_id_type=pl.DeviceIdType.MESH
        )
        return carry

    lax.fori_loop(1, peers, greet, 0)
    own = pltpu.make_async_copy(sent.at[me], held.at[me], own_sem)
    own.start()
    pl.semaphore_wait(barrier, peers - 1)

    def remote(step):
        peer, target = place(step)
        return pltpu.make_async_remote_copy(
            src_ref=sent.at[peer],
            dst_ref=held.at[me],
            send_sem=send_sem.at[step],
            recv_sem=recv_sem.at[step],
            device_id=target,
            device_id_type=pl.DeviceIdType.MESH,
        )

    def launch(step, carry):
        remote(step).start()
        return carry

    def finish(step, carry):
        remote(step).wait()
        return carry

    lax.fori_loop(1, peers, launch, 0)
    own.wait()
    lax.fori_loop(1, peers, finish, 0)


def exchange(blocks, collective_id):
    count, seqs = lax.axis_size("ctx"), lax.axis_size("dp")
    peers, rows, lanes = blocks.shape
    extra = -rows % 16
    if extra:
        blocks = jnp.pad(blocks, ((0, 0), (0, extra), (0, 0)))
    held = pl.pallas_call(
        functools.partial(exchange_kernel, count, seqs),
        out_shape=jax.ShapeDtypeStruct(blocks.shape, blocks.dtype),
        in_specs=[pl.BlockSpec(memory_space=pltpu.VMEM)],
        out_specs=pl.BlockSpec(memory_space=pltpu.VMEM),
        scratch_shapes=[
            pltpu.SemaphoreType.DMA((peers,)),
            pltpu.SemaphoreType.DMA((peers,)),
            pltpu.SemaphoreType.DMA,
        ],
        compiler_params=pltpu.CompilerParams(
            collective_id=collective_id, has_side_effects=True, vmem_limit_bytes=32 * 2**20
        ),
        name="exchange",
    )(blocks)
    return held[:, :rows] if extra else held


def convolve_all(packed, seqs, share):
    outer, columns, _ = packed.shape
    length = outer * LANES
    wide = seqs * share
    tables = dft_tables(length)
    forward_first, inverse_first, forward_second, inverse_second, cos_turn, sin_turn = tables
    high, low = split_table(forward_first)
    flat = packed.reshape(outer, columns * LANES)
    spread = dot(jnp.concatenate([high, low], axis=1), jnp.concatenate([flat, flat], axis=0))
    spread = spread.reshape(2 * outer, columns, LANES)
    real, imag = spread[:outer], spread[outer:]
    both = jnp.concatenate(
        [real * cos_turn + imag * sin_turn, imag * cos_turn - real * sin_turn], axis=2
    ).reshape(outer * columns, 2 * LANES)
    spec = jnp.dot(both, forward_second, precision=lax.Precision.HIGH)
    spec = spec.reshape(outer, columns, 2 * LANES)
    real, imag = spec[:, :, :LANES], spec[:, :, LANES:]
    kernel_real = real[:, 2 * wide :][:, None]
    kernel_imag = imag[:, 2 * wide :][:, None]
    grouped = (outer, seqs, share, LANES)
    value_real = real[:, :wide].reshape(grouped)
    value_imag = imag[:, :wide].reshape(grouped)
    grad_real = real[:, wide : 2 * wide].reshape(grouped)
    grad_imag = imag[:, wide : 2 * wide].reshape(grouped)
    mixed_real = value_real * kernel_real - value_imag * kernel_imag
    mixed_imag = value_real * kernel_imag + value_imag * kernel_real
    back_real = grad_real * kernel_real + grad_imag * kernel_imag
    back_imag = grad_imag * kernel_real - grad_real * kernel_imag
    corr_real = jnp.sum(grad_real * value_real + grad_imag * value_imag, axis=1)
    corr_imag = jnp.sum(grad_imag * value_real - grad_real * value_imag, axis=1)
    narrow = (outer, wide, LANES)
    out_real = jnp.concatenate(
        [mixed_real.reshape(narrow), back_real.reshape(narrow), corr_real], axis=1
    )
    out_imag = jnp.concatenate(
        [mixed_imag.reshape(narrow), back_imag.reshape(narrow), corr_imag], axis=1
    )
    both = jnp.concatenate([out_real, out_imag], axis=2).reshape(outer * columns, 2 * LANES)
    part = jnp.dot(both, inverse_second, precision=lax.Precision.HIGH)
    part = part.reshape(outer, columns, 2 * LANES)
    real, imag = part[:, :, :LANES], part[:, :, LANES:]
    turned = jnp.concatenate(
        [real * cos_turn - imag * sin_turn, imag * cos_turn + real * sin_turn], axis=0
    ).reshape(2 * outer, columns * LANES)
    rows = jnp.dot(inverse_first, turned, precision=lax.Precision.HIGH)
    return rows.reshape(outer, columns, LANES)


def local(inputs, value_weight, gate_weight, output_weight, filters, cotangent):
    token_rows = inputs[0]
    upstream = cotangent[0]
    tok_rows, width = token_rows.shape
    count = lax.axis_size("ctx")
    seqs = lax.axis_size("dp")
    peers = count * seqs
    share = width // peers
    tiles = tok_rows // LANES
    half = tok_rows // seqs
    value_act = contract(value_weight, 0, token_rows, 1).astype(jnp.bfloat16)
    gate_act = contract(gate_weight, 0, token_rows, 1)
    d_gated = contract(output_weight, 1, upstream, 1)
    d_mixed = (d_gated * gate_act).astype(jnp.bfloat16)
    kernel_part = lax.dynamic_slice_in_dim(filters, lax.axis_index("dp") * half, half, 0).T
    sent = jnp.concatenate(
        [
            value_act.reshape(peers, share * tiles, LANES),
            d_mixed.reshape(peers, share * tiles, LANES),
            kernel_part.reshape(peers, share * half // LANES, LANES),
        ],
        axis=1,
    )
    held = exchange(sent, 0)
    cut = share * tiles
    fields = held[:, : 2 * cut].reshape(count, seqs, 2, share, tiles, LANES)
    fields = fields.transpose(0, 4, 2, 1, 3, 5).reshape(count * tiles, 2 * seqs * share, LANES)
    taps = held[:, 2 * cut :].reshape(count, seqs, share, half // LANES, LANES)
    taps = taps.transpose(0, 1, 3, 2, 4).reshape(count * tiles, share, LANES)
    rows = convolve_all(jnp.concatenate([fields, taps], axis=1), seqs, share)
    grad_scale = 1.0 / math.sqrt(seqs * count * tok_rows)
    wide = seqs * share
    fields = rows[:, : 2 * wide].astype(jnp.bfloat16)
    fields = fields.reshape(count, tiles, 2, seqs, share, LANES).transpose(0, 3, 2, 4, 1, 5)
    terms = (rows[:, 2 * wide :] * grad_scale).astype(jnp.bfloat16)
    terms = terms.reshape(count, tiles, share, LANES).transpose(0, 2, 1, 3)
    terms = jnp.broadcast_to(
        terms.reshape(count, 1, share * tiles, LANES), (count, seqs, share * tiles, LANES)
    )
    back = exchange(
        jnp.concatenate(
            [
                fields.reshape(peers, 2 * share * tiles, LANES),
                terms.reshape(peers, share * tiles, LANES),
            ],
            axis=1,
        ),
        1,
    )
    mixed_act = back[:, :cut].reshape(width, tok_rows).astype(jnp.float32)
    d_value = back[:, cut : 2 * cut].reshape(width, tok_rows)
    filter_grads = back[:, 2 * cut :].reshape(width, tok_rows).T.astype(jnp.float32)
    gated = (gate_act * mixed_act).astype(jnp.bfloat16)
    d_gate = (d_gated * mixed_act).astype(jnp.bfloat16)
    input_rows = contract(d_value, 0, value_weight, 1) + contract(d_gate, 0, gate_weight, 1)
    input_grad = input_rows.astype(jnp.bfloat16)[None]
    proj_terms = jnp.stack(
        [
            contract(token_rows, 0, d_value, 1),
            contract(token_rows, 0, d_gate, 1),
            dot(gated, upstream),
        ],
        axis=0,
    )
    proj_terms = (proj_terms * grad_scale).astype(jnp.bfloat16)
    cell = width // count
    proj_terms = proj_terms.reshape(3, count, cell, width).transpose(1, 0, 2, 3)
    proj_terms = jnp.broadcast_to(
        proj_terms.reshape(count, 1, 3 * cell, width), (count, seqs, 3 * cell, width)
    )
    proj_held = exchange(proj_terms.reshape(peers, 3 * cell, width), 2)
    proj_grads = jnp.sum(proj_held.astype(jnp.float32), axis=0).reshape(3, cell, width)
    return (input_grad, proj_grads, filter_grads)


def solution(mesh):
    return jax.shard_map(
        local,
        mesh=mesh,
        in_specs=(
            P(("groups", "dp"), "ctx", None),
            P(),
            P(),
            P(),
            P("ctx", None),
            P(("groups", "dp"), "ctx", None),
        ),
        out_specs=(
            P(("groups", "dp"), "ctx", None),
            P("groups", "ctx", None),
            P(("groups", "ctx"), None),
        ),
        check_vma=False,
    )
```

```python
import functools
import math

import jax
import jax.numpy as jnp
import numpy as np
from jax import lax
from jax.experimental import pallas as pl
from jax.experimental.pallas import tpu as pltpu
from jax.sharding import PartitionSpec as P

LANES = 128
AXES = ("ctx", "dp")


def dft_tables(length):
    outer = length // LANES
    k_outer = np.arange(outer)
    k_inner = np.arange(LANES)
    first = 2.0 * np.pi / outer * (np.outer(k_outer, k_outer) % outer)
    turn = 2.0 * np.pi / length * (np.outer(k_outer, k_inner) % length)
    second = 2.0 * np.pi / LANES * (np.outer(k_inner, k_inner) % LANES)
    cos_first, sin_first = np.cos(first), np.sin(first)
    cos_second, sin_second = np.cos(second), np.sin(second)
    forward_first = np.concatenate([cos_first, -sin_first], axis=0)
    inverse_first = np.concatenate([cos_first, -sin_first], axis=1) / length
    forward_second = np.block([[cos_second, -sin_second], [sin_second, cos_second]])
    inverse_second = np.block([[cos_second, sin_second], [-sin_second, cos_second]])
    as_float = [
        table.astype(np.float32)
        for table in (forward_first, inverse_first, forward_second, inverse_second)
    ]
    cos_turn = np.cos(turn).astype(np.float32)[:, None, :]
    sin_turn = np.sin(turn).astype(np.float32)[:, None, :]
    return as_float + [cos_turn, sin_turn]


def split(value):
    high = value.astype(jnp.bfloat16)
    low = (value - high.astype(jnp.float32)).astype(jnp.bfloat16)
    return high, low


def split_table(table):
    high = table.astype(jnp.bfloat16)
    return high, (table - high.astype(np.float32)).astype(jnp.bfloat16)


def dot(left, right):
    return jnp.dot(left, right, preferred_element_type=jnp.float32)


def contract(left, left_dim, right, right_dim):
    return lax.dot_general(
        left, right, (((left_dim,), (right_dim,)), ((), ())), preferred_element_type=jnp.float32
    )


def exchange_kernel(count, seqs, sent, held, send_sem, recv_sem, own_sem):
    peers = count * seqs
    me = lax.axis_index("ctx") * seqs + lax.axis_index("dp")
    barrier = pltpu.get_barrier_semaphore()

    def place(step):
        peer = lax.rem(me + step, peers)
        return peer, {"ctx": lax.div(peer, seqs), "dp": lax.rem(peer, seqs)}

    def greet(step, carry):
        pl.semaphore_signal(
            barrier, inc=1, device_id=place(step)[1], device_id_type=pl.DeviceIdType.MESH
        )
        return carry

    lax.fori_loop(1, peers, greet, 0)
    own = pltpu.make_async_copy(sent.at[me], held.at[me], own_sem)
    own.start()
    pl.semaphore_wait(barrier, peers - 1)

    def remote(step):
        peer, target = place(step)
        return pltpu.make_async_remote_copy(
            src_ref=sent.at[peer],
            dst_ref=held.at[me],
            send_sem=send_sem.at[step],
            recv_sem=recv_sem.at[step],
            device_id=target,
            device_id_type=pl.DeviceIdType.MESH,
        )

    def launch(step, carry):
        remote(step).start()
        return carry

    def finish(step, carry):
        remote(step).wait()
        return carry

    lax.fori_loop(1, peers, launch, 0)
    own.wait()
    lax.fori_loop(1, peers, finish, 0)


def exchange(blocks, collective_id):
    count, seqs = lax.axis_size("ctx"), lax.axis_size("dp")
    peers, rows, lanes = blocks.shape
    extra = -rows % 16
    if extra:
        blocks = jnp.pad(blocks, ((0, 0), (0, extra), (0, 0)))
    held = pl.pallas_call(
        functools.partial(exchange_kernel, count, seqs),
        out_shape=jax.ShapeDtypeStruct(blocks.shape, blocks.dtype),
        in_specs=[pl.BlockSpec(memory_space=pltpu.VMEM)],
        out_specs=pl.BlockSpec(memory_space=pltpu.VMEM),
        scratch_shapes=[
            pltpu.SemaphoreType.DMA((peers,)),
            pltpu.SemaphoreType.DMA((peers,)),
            pltpu.SemaphoreType.DMA,
        ],
        compiler_params=pltpu.CompilerParams(
            collective_id=collective_id, has_side_effects=True, vmem_limit_bytes=32 * 2**20
        ),
        name="exchange",
    )(blocks)
    return held[:, :rows] if extra else held


def reduce_kernel(count, proj, terms, sums, all_terms, other, stage, held, send_sem, recv_sem, go_sem, come_sem):
    place = lax.axis_index("ctx")
    core = lax.axis_index("dp")
    barrier = pltpu.get_barrier_semaphore()

    def send(source, target, slot):
        return pltpu.make_async_remote_copy(
            src_ref=source,
            dst_ref=target,
            send_sem=send_sem.at[slot],
            recv_sem=recv_sem.at[slot],
            device_id={"dp": 1 - core},
            device_id_type=pl.DeviceIdType.MESH,
        )

    def across(step):
        peer = lax.rem(place + step, count)
        return pltpu.make_async_remote_copy(
            src_ref=stage.at[peer],
            dst_ref=held.at[place],
            send_sem=go_sem.at[step],
            recv_sem=come_sem.at[step],
            device_id={"ctx": peer},
            device_id_type=pl.DeviceIdType.MESH,
        )

    def greet(step, carry):
        pl.semaphore_signal(
            barrier,
            inc=1,
            device_id={"ctx": lax.rem(place + step, count)},
            device_id_type=pl.DeviceIdType.MESH,
        )
        return carry

    def launch(step, carry):
        across(step).start()
        return carry

    def finish(step, carry):
        across(step).wait()
        return carry

    def add(step, total):
        return total + held[lax.rem(place + step, count)].astype(jnp.float32)

    pl.semaphore_signal(
        barrier, inc=1, device_id={"dp": 1 - core}, device_id_type=pl.DeviceIdType.MESH
    )
    lax.fori_loop(1, count, greet, 0)
    pl.semaphore_wait(barrier, count)
    halves = send(proj.at[1 - core], other, 0)
    halves.start()
    taps = send(terms, all_terms.at[core], 1)
    taps.start()
    all_terms[core] = terms[...]
    halves.wait()
    stage[...] = (proj[core].astype(jnp.float32) + other[...].astype(jnp.float32)).astype(
        jnp.bfloat16
    )
    lax.fori_loop(1, count, launch, 0)
    taps.wait()
    lax.fori_loop(1, count, finish, 0)
    sums[core] = lax.fori_loop(1, count, add, stage[place].astype(jnp.float32))
    total = send(sums.at[core], sums.at[core], 2)
    total.start()
    total.wait()


def reduce_and_join(proj, terms, collective_id):
    count = lax.axis_size("ctx")
    rows = proj.shape[2]
    extra = -rows % 16
    if extra:
        proj = jnp.pad(proj, ((0, 0), (0, 0), (0, extra), (0, 0)))
    part = proj.shape[1:]
    sums, all_terms = pl.pallas_call(
        functools.partial(reduce_kernel, count),
        out_shape=(
            jax.ShapeDtypeStruct((2,) + part[1:], jnp.float32),
            jax.ShapeDtypeStruct((2,) + terms.shape, terms.dtype),
        ),
        in_specs=[pl.BlockSpec(memory_space=pltpu.VMEM)] * 2,
        out_specs=(pl.BlockSpec(memory_space=pltpu.VMEM),) * 2,
        scratch_shapes=[
            pltpu.VMEM(part, jnp.bfloat16),
            pltpu.VMEM(part, jnp.bfloat16),
            pltpu.VMEM(part, jnp.bfloat16),
            pltpu.SemaphoreType.DMA((3,)),
            pltpu.SemaphoreType.DMA((3,)),
            pltpu.SemaphoreType.DMA((count,)),
            pltpu.SemaphoreType.DMA((count,)),
        ],
        compiler_params=pltpu.CompilerParams(
            collective_id=collective_id, has_side_effects=True, vmem_limit_bytes=32 * 2**20
        ),
        name="reduce_and_join",
    )(proj, terms)
    return sums[:, :rows], all_terms


def convolve_all(packed, seqs, share):
    outer, columns, _ = packed.shape
    length = outer * LANES
    wide = seqs * share
    tables = dft_tables(length)
    forward_first, inverse_first, forward_second, inverse_second, cos_turn, sin_turn = tables
    high, low = split_table(forward_first)
    flat = packed.reshape(outer, columns * LANES)
    spread = dot(jnp.concatenate([high, low], axis=1), jnp.concatenate([flat, flat], axis=0))
    spread = spread.reshape(2 * outer, columns, LANES)
    real, imag = spread[:outer], spread[outer:]
    both = jnp.concatenate(
        [real * cos_turn + imag * sin_turn, imag * cos_turn - real * sin_turn], axis=2
    ).reshape(outer * columns, 2 * LANES)
    spec = jnp.dot(both, forward_second, precision=lax.Precision.HIGH)
    spec = spec.reshape(outer, columns, 2 * LANES)
    real, imag = spec[:, :, :LANES], spec[:, :, LANES:]
    kernel_real = real[:, 2 * wide :][:, None]
    kernel_imag = imag[:, 2 * wide :][:, None]
    grouped = (outer, seqs, share, LANES)
    value_real = real[:, :wide].reshape(grouped)
    value_imag = imag[:, :wide].reshape(grouped)
    grad_real = real[:, wide : 2 * wide].reshape(grouped)
    grad_imag = imag[:, wide : 2 * wide].reshape(grouped)
    mixed_real = value_real * kernel_real - value_imag * kernel_imag
    mixed_imag = value_real * kernel_imag + value_imag * kernel_real
    back_real = grad_real * kernel_real + grad_imag * kernel_imag
    back_imag = grad_imag * kernel_real - grad_real * kernel_imag
    corr_real = jnp.sum(grad_real * value_real + grad_imag * value_imag, axis=1)
    corr_imag = jnp.sum(grad_imag * value_real - grad_real * value_imag, axis=1)
    narrow = (outer, wide, LANES)
    out_real = jnp.concatenate(
        [mixed_real.reshape(narrow), back_real.reshape(narrow), corr_real], axis=1
    )
    out_imag = jnp.concatenate(
        [mixed_imag.reshape(narrow), back_imag.reshape(narrow), corr_imag], axis=1
    )
    both = jnp.concatenate([out_real, out_imag], axis=2).reshape(outer * columns, 2 * LANES)
    part = jnp.dot(both, inverse_second, precision=lax.Precision.HIGH)
    part = part.reshape(outer, columns, 2 * LANES)
    real, imag = part[:, :, :LANES], part[:, :, LANES:]
    turned = jnp.concatenate(
        [real * cos_turn - imag * sin_turn, imag * cos_turn + real * sin_turn], axis=0
    ).reshape(2 * outer, columns * LANES)
    rows = jnp.dot(inverse_first, turned, precision=lax.Precision.HIGH)
    return rows.reshape(outer, columns, LANES)


def local(inputs, value_weight, gate_weight, output_weight, filters, cotangent):
    token_rows = inputs[0]
    upstream = cotangent[0]
    tok_rows, width = token_rows.shape
    count = lax.axis_size("ctx")
    seqs = lax.axis_size("dp")
    peers = count * seqs
    share = width // peers
    tiles = tok_rows // LANES
    half = tok_rows // seqs
    value_act = contract(value_weight, 0, token_rows, 1).astype(jnp.bfloat16)
    gate_act = contract(gate_weight, 0, token_rows, 1)
    d_gated = contract(output_weight, 1, upstream, 1)
    d_mixed = (d_gated * gate_act).astype(jnp.bfloat16)
    kernel_part = lax.dynamic_slice_in_dim(filters, lax.axis_index("dp") * half, half, 0).T
    sent = jnp.concatenate(
        [
            value_act.reshape(peers, share * tiles, LANES),
            d_mixed.reshape(peers, share * tiles, LANES),
            kernel_part.reshape(peers, share * half // LANES, LANES),
        ],
        axis=1,
    )
    held = exchange(sent, 0)
    cut = share * tiles
    fields = held[:, : 2 * cut].reshape(count, seqs, 2, share, tiles, LANES)
    fields = fields.transpose(0, 4, 2, 1, 3, 5).reshape(count * tiles, 2 * seqs * share, LANES)
    taps = held[:, 2 * cut :].reshape(count, seqs, share, half // LANES, LANES)
    taps = taps.transpose(0, 1, 3, 2, 4).reshape(count * tiles, share, LANES)
    rows = convolve_all(jnp.concatenate([fields, taps], axis=1), seqs, share)
    grad_scale = 1.0 / math.sqrt(seqs * count * tok_rows)
    wide = seqs * share
    fields = rows[:, : 2 * wide].astype(jnp.bfloat16)
    fields = fields.reshape(count, tiles, 2, seqs, share, LANES).transpose(0, 3, 2, 4, 1, 5)
    terms = (rows[:, 2 * wide :] * grad_scale).astype(jnp.bfloat16)
    near = tiles // seqs
    terms = terms.reshape(count, seqs, near, share, LANES).transpose(0, 1, 3, 2, 4)
    back = exchange(
        jnp.concatenate(
            [
                fields.reshape(peers, 2 * share * tiles, LANES),
                terms.reshape(peers, share * near, LANES),
            ],
            axis=1,
        ),
        1,
    )
    mixed_act = back[:, :cut].reshape(width, tok_rows).astype(jnp.float32)
    d_value = back[:, cut : 2 * cut].reshape(width, tok_rows)
    gated = (gate_act * mixed_act).astype(jnp.bfloat16)
    d_gate = (d_gated * mixed_act).astype(jnp.bfloat16)
    input_rows = contract(d_value, 0, value_weight, 1) + contract(d_gate, 0, gate_weight, 1)
    input_grad = input_rows.astype(jnp.bfloat16)[None]
    proj_terms = jnp.stack(
        [
            contract(token_rows, 0, d_value, 1),
            contract(token_rows, 0, d_gate, 1),
            dot(gated, upstream),
        ],
        axis=0,
    )
    proj_terms = (proj_terms * grad_scale).astype(jnp.bfloat16)
    cell = width // count
    part = cell // seqs
    pack = width // LANES
    proj_terms = proj_terms.reshape(3, count, seqs, part, width).transpose(2, 1, 0, 3, 4)
    proj_sums, all_terms = reduce_and_join(
        proj_terms.reshape(seqs, count, 3 * part * pack, LANES),
        back[:, 2 * cut :].reshape(width * near, LANES),
        2,
    )
    proj_grads = proj_sums.reshape(seqs, 3, part, width).transpose(1, 0, 2, 3)
    proj_grads = proj_grads.reshape(3, cell, width)
    filter_grads = all_terms.reshape(seqs, width, half).transpose(0, 2, 1)
    filter_grads = filter_grads.reshape(tok_rows, width).astype(jnp.float32)
    return (input_grad, proj_grads, filter_grads)


def solution(mesh):
    return jax.shard_map(
        local,
        mesh=mesh,
        in_specs=(
            P(("groups", "dp"), "ctx", None),
            P(),
            P(),
            P(),
            P("ctx", None),
            P(("groups", "dp"), "ctx", None),
        ),
        out_specs=(
            P(("groups", "dp"), "ctx", None),
            P("groups", "ctx", None),
            P(("groups", "ctx"), None),
        ),
        check_vma=False,
    )
```

```python
import functools
import math

import jax
import jax.numpy as jnp
import numpy as np
from jax import lax
from jax.experimental import pallas as pl
from jax.experimental.pallas import tpu as pltpu
from jax.sharding import PartitionSpec as P

LANES = 128
AXES = ("ctx", "dp")


def dft_tables(length):
    outer = length // LANES
    k_outer = np.arange(outer)
    k_inner = np.arange(LANES)
    first = 2.0 * np.pi / outer * (np.outer(k_outer, k_outer) % outer)
    turn = 2.0 * np.pi / length * (np.outer(k_outer, k_inner) % length)
    second = 2.0 * np.pi / LANES * (np.outer(k_inner, k_inner) % LANES)
    cos_first, sin_first = np.cos(first), np.sin(first)
    cos_second, sin_second = np.cos(second), np.sin(second)
    forward_first = np.concatenate([cos_first, -sin_first], axis=0)
    inverse_first = np.concatenate([cos_first, -sin_first], axis=1) / length
    forward_second = np.block([[cos_second, -sin_second], [sin_second, cos_second]])
    inverse_second = np.block([[cos_second, sin_second], [-sin_second, cos_second]])
    as_float = [
        table.astype(np.float32)
        for table in (forward_first, inverse_first, forward_second, inverse_second)
    ]
    cos_turn = np.cos(turn).astype(np.float32)[:, None, :]
    sin_turn = np.sin(turn).astype(np.float32)[:, None, :]
    return as_float + [cos_turn, sin_turn]


def split(value):
    high = value.astype(jnp.bfloat16)
    low = (value - high.astype(jnp.float32)).astype(jnp.bfloat16)
    return high, low


def split_table(table):
    high = table.astype(jnp.bfloat16)
    return high, (table - high.astype(np.float32)).astype(jnp.bfloat16)


def dot(left, right):
    return jnp.dot(left, right, preferred_element_type=jnp.float32)


def contract(left, left_dim, right, right_dim):
    return lax.dot_general(
        left, right, (((left_dim,), (right_dim,)), ((), ())), preferred_element_type=jnp.float32
    )


def exchange_kernel(count, seqs, sent, held, send_sem, recv_sem, own_sem):
    peers = count * seqs
    me = lax.axis_index("ctx") * seqs + lax.axis_index("dp")
    barrier = pltpu.get_barrier_semaphore()

    def place(step):
        peer = lax.rem(me + step, peers)
        return peer, {"ctx": lax.div(peer, seqs), "dp": lax.rem(peer, seqs)}

    def greet(step, carry):
        pl.semaphore_signal(
            barrier, inc=1, device_id=place(step)[1], device_id_type=pl.DeviceIdType.MESH
        )
        return carry

    lax.fori_loop(1, peers, greet, 0)
    own = pltpu.make_async_copy(sent.at[me], held.at[me], own_sem)
    own.start()
    pl.semaphore_wait(barrier, peers - 1)

    def remote(step):
        peer, target = place(step)
        return pltpu.make_async_remote_copy(
            src_ref=sent.at[peer],
            dst_ref=held.at[me],
            send_sem=send_sem.at[step],
            recv_sem=recv_sem.at[step],
            device_id=target,
            device_id_type=pl.DeviceIdType.MESH,
        )

    def launch(step, carry):
        remote(step).start()
        return carry

    def finish(step, carry):
        remote(step).wait()
        return carry

    lax.fori_loop(1, peers, launch, 0)
    own.wait()
    lax.fori_loop(1, peers, finish, 0)


def exchange(blocks, collective_id):
    count, seqs = lax.axis_size("ctx"), lax.axis_size("dp")
    peers, rows, lanes = blocks.shape
    extra = -rows % 16
    if extra:
        blocks = jnp.pad(blocks, ((0, 0), (0, extra), (0, 0)))
    held = pl.pallas_call(
        functools.partial(exchange_kernel, count, seqs),
        out_shape=jax.ShapeDtypeStruct(blocks.shape, blocks.dtype),
        in_specs=[pl.BlockSpec(memory_space=pltpu.VMEM)],
        out_specs=pl.BlockSpec(memory_space=pltpu.VMEM),
        scratch_shapes=[
            pltpu.SemaphoreType.DMA((peers,)),
            pltpu.SemaphoreType.DMA((peers,)),
            pltpu.SemaphoreType.DMA,
        ],
        compiler_params=pltpu.CompilerParams(
            collective_id=collective_id, has_side_effects=True, vmem_limit_bytes=32 * 2**20
        ),
        name="exchange",
    )(blocks)
    return held[:, :rows] if extra else held


def reduce_kernel(count, proj, terms, sums, all_terms, other, stage, held, send_sem, recv_sem, go_sem, come_sem):
    place = lax.axis_index("ctx")
    core = lax.axis_index("dp")
    barrier = pltpu.get_barrier_semaphore()

    def send(source, target, slot):
        return pltpu.make_async_remote_copy(
            src_ref=source,
            dst_ref=target,
            send_sem=send_sem.at[slot],
            recv_sem=recv_sem.at[slot],
            device_id={"dp": 1 - core},
            device_id_type=pl.DeviceIdType.MESH,
        )

    def across(step):
        peer = lax.rem(place + step, count)
        return pltpu.make_async_remote_copy(
            src_ref=stage.at[peer],
            dst_ref=held.at[place],
            send_sem=go_sem.at[step],
            recv_sem=come_sem.at[step],
            device_id={"ctx": peer},
            device_id_type=pl.DeviceIdType.MESH,
        )

    def greet(step, carry):
        pl.semaphore_signal(
            barrier,
            inc=1,
            device_id={"ctx": lax.rem(place + step, count)},
            device_id_type=pl.DeviceIdType.MESH,
        )
        return carry

    def launch(step, carry):
        across(step).start()
        return carry

    def finish(step, carry):
        across(step).wait()
        return carry

    def add(step, total):
        return total + held[lax.rem(place + step, count)].astype(jnp.float32)

    pl.semaphore_signal(
        barrier, inc=1, device_id={"dp": 1 - core}, device_id_type=pl.DeviceIdType.MESH
    )
    lax.fori_loop(1, count, greet, 0)
    pl.semaphore_wait(barrier, count)
    halves = send(proj.at[1 - core], other, 0)
    halves.start()
    taps = send(terms, all_terms.at[core], 1)
    taps.start()
    all_terms[core] = terms[...]
    halves.wait()
    stage[...] = (proj[core].astype(jnp.float32) + other[...].astype(jnp.float32)).astype(
        jnp.bfloat16
    )
    lax.fori_loop(1, count, launch, 0)
    taps.wait()
    lax.fori_loop(1, count, finish, 0)
    sums[core] = lax.fori_loop(1, count, add, stage[place].astype(jnp.float32))
    total = send(sums.at[core], sums.at[core], 2)
    total.start()
    total.wait()


def reduce_and_join(proj, terms, collective_id):
    count = lax.axis_size("ctx")
    rows = proj.shape[2]
    extra = -rows % 16
    if extra:
        proj = jnp.pad(proj, ((0, 0), (0, 0), (0, extra), (0, 0)))
    part = proj.shape[1:]
    sums, all_terms = pl.pallas_call(
        functools.partial(reduce_kernel, count),
        out_shape=(
            jax.ShapeDtypeStruct((2,) + part[1:], jnp.float32),
            jax.ShapeDtypeStruct((2,) + terms.shape, terms.dtype),
        ),
        in_specs=[pl.BlockSpec(memory_space=pltpu.VMEM)] * 2,
        out_specs=(pl.BlockSpec(memory_space=pltpu.VMEM),) * 2,
        scratch_shapes=[
            pltpu.VMEM(part, jnp.bfloat16),
            pltpu.VMEM(part, jnp.bfloat16),
            pltpu.VMEM(part, jnp.bfloat16),
            pltpu.SemaphoreType.DMA((3,)),
            pltpu.SemaphoreType.DMA((3,)),
            pltpu.SemaphoreType.DMA((count,)),
            pltpu.SemaphoreType.DMA((count,)),
        ],
        compiler_params=pltpu.CompilerParams(
            collective_id=collective_id, has_side_effects=True, vmem_limit_bytes=32 * 2**20
        ),
        name="reduce_and_join",
    )(proj, terms)
    return sums[:, :rows], all_terms


def stack_table(table):
    high, low = split_table(table)
    return jnp.concatenate([high, high, low], axis=0)


def spectra_kernel(seqs, share, spread, cos_ref, sin_ref, forward, inverse, turned):
    outer = spread.shape[0] // 2
    columns = spread.shape[1]
    wide = seqs * share
    chunk = 8

    def times(real, imag, table):
        both = jnp.concatenate([real, imag], axis=2).reshape(chunk * columns, 2 * LANES)
        high, low = split(both)
        out = dot(jnp.concatenate([high, low, high], axis=1), table[...])
        out = out.reshape(chunk, columns, 2 * LANES)
        return out[:, :, :LANES], out[:, :, LANES:]

    def step(index, carry):
        first = pl.multiple_of(index * chunk, chunk)
        upper, lower = pl.ds(first, chunk), pl.ds(outer + first, chunk)
        cos_turn, sin_turn = cos_ref[upper], sin_ref[upper]
        real, imag = spread[upper], spread[lower]
        real, imag = times(
            real * cos_turn + imag * sin_turn, imag * cos_turn - real * sin_turn, forward
        )
        kernel_real, kernel_imag = real[:, 2 * wide :], imag[:, 2 * wide :]
        mixed_reals, mixed_imags, back_reals, back_imags = [], [], [], []
        corr_real, corr_imag = 0.0, 0.0
        for seq in range(seqs):
            near = slice(seq * share, (seq + 1) * share)
            far = slice(wide + seq * share, wide + (seq + 1) * share)
            value_real, value_imag = real[:, near], imag[:, near]
            grad_real, grad_imag = real[:, far], imag[:, far]
            mixed_reals.append(value_real * kernel_real - value_imag * kernel_imag)
            mixed_imags.append(value_real * kernel_imag + value_imag * kernel_real)
            back_reals.append(grad_real * kernel_real + grad_imag * kernel_imag)
            back_imags.append(grad_imag * kernel_real - grad_real * kernel_imag)
            corr_real = corr_real + grad_real * value_real + grad_imag * value_imag
            corr_imag = corr_imag + grad_imag * value_real - grad_real * value_imag
        real, imag = times(
            jnp.concatenate(mixed_reals + back_reals + [corr_real], axis=1),
            jnp.concatenate(mixed_imags + back_imags + [corr_imag], axis=1),
            inverse,
        )
        turned[upper] = real * cos_turn - imag * sin_turn
        turned[lower] = imag * cos_turn + real * sin_turn
        return carry

    lax.fori_loop(0, outer // chunk, step, 0)


def convolve_all(packed, seqs, share):
    outer, columns, _ = packed.shape
    length = outer * LANES
    wide = seqs * share
    tables = dft_tables(length)
    forward_first, inverse_first, forward_second, inverse_second, cos_turn, sin_turn = tables
    high, low = split_table(forward_first)
    flat = packed.reshape(outer, columns * LANES)
    spread = dot(jnp.concatenate([high, low], axis=1), jnp.concatenate([flat, flat], axis=0))
    spread = spread.reshape(2 * outer, columns, LANES)
    turned = pl.pallas_call(
        functools.partial(spectra_kernel, seqs, share),
        out_shape=jax.ShapeDtypeStruct(spread.shape, jnp.float32),
        in_specs=[pl.BlockSpec(memory_space=pltpu.VMEM)] * 5,
        out_specs=pl.BlockSpec(memory_space=pltpu.VMEM),
        compiler_params=pltpu.CompilerParams(vmem_limit_bytes=48 * 2**20),
        name="spectra",
    )(spread, cos_turn, sin_turn, stack_table(forward_second), stack_table(inverse_second))
    turned = turned.reshape(2 * outer, columns * LANES)
    rows = jnp.dot(inverse_first, turned, precision=lax.Precision.HIGH)
    return rows.reshape(outer, columns, LANES)


def local(inputs, value_weight, gate_weight, output_weight, filters, cotangent):
    token_rows = inputs[0]
    upstream = cotangent[0]
    tok_rows, width = token_rows.shape
    count = lax.axis_size("ctx")
    seqs = lax.axis_size("dp")
    peers = count * seqs
    share = width // peers
    tiles = tok_rows // LANES
    half = tok_rows // seqs
    value_act = contract(value_weight, 0, token_rows, 1).astype(jnp.bfloat16)
    gate_act = contract(gate_weight, 0, token_rows, 1)
    d_gated = contract(output_weight, 1, upstream, 1)
    d_mixed = (d_gated * gate_act).astype(jnp.bfloat16)
    kernel_part = lax.dynamic_slice_in_dim(filters, lax.axis_index("dp") * half, half, 0).T
    sent = jnp.concatenate(
        [
            value_act.reshape(peers, share * tiles, LANES),
            d_mixed.reshape(peers, share * tiles, LANES),
            kernel_part.reshape(peers, share * half // LANES, LANES),
        ],
        axis=1,
    )
    held = exchange(sent, 0)
    cut = share * tiles
    fields = held[:, : 2 * cut].reshape(count, seqs, 2, share, tiles, LANES)
    fields = fields.transpose(0, 4, 2, 1, 3, 5).reshape(count * tiles, 2 * seqs * share, LANES)
    taps = held[:, 2 * cut :].reshape(count, seqs, share, half // LANES, LANES)
    taps = taps.transpose(0, 1, 3, 2, 4).reshape(count * tiles, share, LANES)
    rows = convolve_all(jnp.concatenate([fields, taps], axis=1), seqs, share)
    grad_scale = 1.0 / math.sqrt(seqs * count * tok_rows)
    wide = seqs * share
    fields = rows[:, : 2 * wide].astype(jnp.bfloat16)
    fields = fields.reshape(count, tiles, 2, seqs, share, LANES).transpose(0, 3, 2, 4, 1, 5)
    terms = (rows[:, 2 * wide :] * grad_scale).astype(jnp.bfloat16)
    near = tiles // seqs
    terms = terms.reshape(count, seqs, near, share, LANES).transpose(0, 1, 3, 2, 4)
    back = exchange(
        jnp.concatenate(
            [
                fields.reshape(peers, 2 * share * tiles, LANES),
                terms.reshape(peers, share * near, LANES),
            ],
            axis=1,
        ),
        1,
    )
    mixed_act = back[:, :cut].reshape(width, tok_rows).astype(jnp.float32)
    d_value = back[:, cut : 2 * cut].reshape(width, tok_rows)
    gated = (gate_act * mixed_act).astype(jnp.bfloat16)
    d_gate = (d_gated * mixed_act).astype(jnp.bfloat16)
    input_rows = contract(d_value, 0, value_weight, 1) + contract(d_gate, 0, gate_weight, 1)
    input_grad = input_rows.astype(jnp.bfloat16)[None]
    proj_terms = jnp.stack(
        [
            contract(token_rows, 0, d_value, 1),
            contract(token_rows, 0, d_gate, 1),
            dot(gated, upstream),
        ],
        axis=0,
    )
    proj_terms = (proj_terms * grad_scale).astype(jnp.bfloat16)
    cell = width // count
    part = cell // seqs
    pack = width // LANES
    proj_terms = proj_terms.reshape(3, count, seqs, part, width).transpose(2, 1, 0, 3, 4)
    proj_sums, all_terms = reduce_and_join(
        proj_terms.reshape(seqs, count, 3 * part * pack, LANES),
        back[:, 2 * cut :].reshape(width * near, LANES),
        2,
    )
    proj_grads = proj_sums.reshape(seqs, 3, part, width).transpose(1, 0, 2, 3)
    proj_grads = proj_grads.reshape(3, cell, width)
    filter_grads = all_terms.reshape(seqs, width, half).transpose(0, 2, 1)
    filter_grads = filter_grads.reshape(tok_rows, width).astype(jnp.float32)
    return (input_grad, proj_grads, filter_grads)


def solution(mesh):
    return jax.shard_map(
        local,
        mesh=mesh,
        in_specs=(
            P(("groups", "dp"), "ctx", None),
            P(),
            P(),
            P(),
            P("ctx", None),
            P(("groups", "dp"), "ctx", None),
        ),
        out_specs=(
            P(("groups", "dp"), "ctx", None),
            P("groups", "ctx", None),
            P(("groups", "ctx"), None),
        ),
        check_vma=False,
    )
```

```python
import functools
import math

import jax
import jax.numpy as jnp
import numpy as np
from jax import lax
from jax.experimental import pallas as pl
from jax.experimental.pallas import tpu as pltpu
from jax.sharding import PartitionSpec as P

LANES = 128
AXES = ("ctx", "dp")


def dft_tables(length):
    outer = length // LANES
    k_outer = np.arange(outer)
    k_inner = np.arange(LANES)
    first = 2.0 * np.pi / outer * (np.outer(k_outer, k_outer) % outer)
    turn = 2.0 * np.pi / length * (np.outer(k_outer, k_inner) % length)
    second = 2.0 * np.pi / LANES * (np.outer(k_inner, k_inner) % LANES)
    cos_first, sin_first = np.cos(first), np.sin(first)
    cos_second, sin_second = np.cos(second), np.sin(second)
    forward_first = np.concatenate([cos_first, -sin_first], axis=0)
    inverse_first = np.concatenate([cos_first, -sin_first], axis=1) / length
    forward_second = np.block([[cos_second, -sin_second], [sin_second, cos_second]])
    inverse_second = np.block([[cos_second, sin_second], [-sin_second, cos_second]])
    as_float = [
        table.astype(np.float32)
        for table in (forward_first, inverse_first, forward_second, inverse_second)
    ]
    cos_turn = np.cos(turn).astype(np.float32)[:, None, :]
    sin_turn = np.sin(turn).astype(np.float32)[:, None, :]
    return as_float + [cos_turn, sin_turn]


def split(value):
    high = value.astype(jnp.bfloat16)
    low = (value - high.astype(jnp.float32)).astype(jnp.bfloat16)
    return high, low


def split_table(table):
    high = table.astype(jnp.bfloat16)
    return high, (table - high.astype(np.float32)).astype(jnp.bfloat16)


def dot(left, right):
    return jnp.dot(left, right, preferred_element_type=jnp.float32)


def contract(left, left_dim, right, right_dim):
    return lax.dot_general(
        left, right, (((left_dim,), (right_dim,)), ((), ())), preferred_element_type=jnp.float32
    )


def exchange_kernel(count, seqs, sent, held, send_sem, recv_sem, own_sem):
    peers = count * seqs
    me = lax.axis_index("ctx") * seqs + lax.axis_index("dp")
    barrier = pltpu.get_barrier_semaphore()

    def place(step):
        peer = lax.rem(me + step, peers)
        return peer, {"ctx": lax.div(peer, seqs), "dp": lax.rem(peer, seqs)}

    def greet(step, carry):
        pl.semaphore_signal(
            barrier, inc=1, device_id=place(step)[1], device_id_type=pl.DeviceIdType.MESH
        )
        return carry

    lax.fori_loop(1, peers, greet, 0)
    own = pltpu.make_async_copy(sent.at[me], held.at[me], own_sem)
    own.start()
    pl.semaphore_wait(barrier, peers - 1)

    def remote(step):
        peer, target = place(step)
        return pltpu.make_async_remote_copy(
            src_ref=sent.at[peer],
            dst_ref=held.at[me],
            send_sem=send_sem.at[step],
            recv_sem=recv_sem.at[step],
            device_id=target,
            device_id_type=pl.DeviceIdType.MESH,
        )

    def launch(turn, carry):
        away = lax.div(turn + 1, 2) * (1 - 2 * lax.rem(turn, 2))
        remote(peers // 2 + away).start()
        return carry

    def finish(step, carry):
        remote(step).wait()
        return carry

    lax.fori_loop(0, peers - 1, launch, 0)
    own.wait()
    lax.fori_loop(1, peers, finish, 0)


def exchange(blocks, collective_id):
    count, seqs = lax.axis_size("ctx"), lax.axis_size("dp")
    peers, rows, lanes = blocks.shape
    extra = -rows % 16
    if extra:
        blocks = jnp.pad(blocks, ((0, 0), (0, extra), (0, 0)))
    held = pl.pallas_call(
        functools.partial(exchange_kernel, count, seqs),
        out_shape=jax.ShapeDtypeStruct(blocks.shape, blocks.dtype),
        in_specs=[pl.BlockSpec(memory_space=pltpu.VMEM)],
        out_specs=pl.BlockSpec(memory_space=pltpu.VMEM),
        scratch_shapes=[
            pltpu.SemaphoreType.DMA((peers,)),
            pltpu.SemaphoreType.DMA((peers,)),
            pltpu.SemaphoreType.DMA,
        ],
        compiler_params=pltpu.CompilerParams(
            collective_id=collective_id, has_side_effects=True, vmem_limit_bytes=32 * 2**20
        ),
        name="exchange",
    )(blocks)
    return held[:, :rows] if extra else held


def reduce_kernel(count, proj, terms, sums, all_terms, other, stage, held, send_sem, recv_sem, go_sem, come_sem):
    place = lax.axis_index("ctx")
    core = lax.axis_index("dp")
    barrier = pltpu.get_barrier_semaphore()

    def send(source, target, slot):
        return pltpu.make_async_remote_copy(
            src_ref=source,
            dst_ref=target,
            send_sem=send_sem.at[slot],
            recv_sem=recv_sem.at[slot],
            device_id={"dp": 1 - core},
            device_id_type=pl.DeviceIdType.MESH,
        )

    def across(step):
        peer = lax.rem(place + step, count)
        return pltpu.make_async_remote_copy(
            src_ref=stage.at[peer],
            dst_ref=held.at[place],
            send_sem=go_sem.at[step],
            recv_sem=come_sem.at[step],
            device_id={"ctx": peer},
            device_id_type=pl.DeviceIdType.MESH,
        )

    def greet(step, carry):
        pl.semaphore_signal(
            barrier,
            inc=1,
            device_id={"ctx": lax.rem(place + step, count)},
            device_id_type=pl.DeviceIdType.MESH,
        )
        return carry

    def launch(step, carry):
        across(step).start()
        return carry

    def finish(step, carry):
        across(step).wait()
        return carry

    def add(step, total):
        return total + held[lax.rem(place + step, count)].astype(jnp.float32)

    pl.semaphore_signal(
        barrier, inc=1, device_id={"dp": 1 - core}, device_id_type=pl.DeviceIdType.MESH
    )
    lax.fori_loop(1, count, greet, 0)
    pl.semaphore_wait(barrier, count)
    halves = send(proj.at[1 - core], other, 0)
    halves.start()
    taps = send(terms, all_terms.at[core], 1)
    taps.start()
    all_terms[core] = terms[...]
    halves.wait()
    stage[...] = (proj[core].astype(jnp.float32) + other[...].astype(jnp.float32)).astype(
        jnp.bfloat16
    )
    lax.fori_loop(1, count, launch, 0)
    taps.wait()
    lax.fori_loop(1, count, finish, 0)
    sums[core] = lax.fori_loop(1, count, add, stage[place].astype(jnp.float32))
    total = send(sums.at[core], sums.at[core], 2)
    total.start()
    total.wait()


def reduce_and_join(proj, terms, collective_id):
    count = lax.axis_size("ctx")
    rows = proj.shape[2]
    extra = -rows % 16
    if extra:
        proj = jnp.pad(proj, ((0, 0), (0, 0), (0, extra), (0, 0)))
    part = proj.shape[1:]
    sums, all_terms = pl.pallas_call(
        functools.partial(reduce_kernel, count),
        out_shape=(
            jax.ShapeDtypeStruct((2,) + part[1:], jnp.float32),
            jax.ShapeDtypeStruct((2,) + terms.shape, terms.dtype),
        ),
        in_specs=[pl.BlockSpec(memory_space=pltpu.VMEM)] * 2,
        out_specs=(pl.BlockSpec(memory_space=pltpu.VMEM),) * 2,
        scratch_shapes=[
            pltpu.VMEM(part, jnp.bfloat16),
            pltpu.VMEM(part, jnp.bfloat16),
            pltpu.VMEM(part, jnp.bfloat16),
            pltpu.SemaphoreType.DMA((3,)),
            pltpu.SemaphoreType.DMA((3,)),
            pltpu.SemaphoreType.DMA((count,)),
            pltpu.SemaphoreType.DMA((count,)),
        ],
        compiler_params=pltpu.CompilerParams(
            collective_id=collective_id, has_side_effects=True, vmem_limit_bytes=32 * 2**20
        ),
        name="reduce_and_join",
    )(proj, terms)
    return sums[:, :rows], all_terms


def stack_table(table):
    high, low = split_table(table)
    return jnp.concatenate([high, high, low], axis=0)


def spectra_kernel(seqs, share, spread, cos_ref, sin_ref, forward, inverse, turned):
    outer = spread.shape[0] // 2
    columns = spread.shape[1]
    wide = seqs * share
    chunk = 8

    def times(real, imag, table):
        both = jnp.concatenate([real, imag], axis=2).reshape(chunk * columns, 2 * LANES)
        high, low = split(both)
        out = dot(jnp.concatenate([high, low, high], axis=1), table[...])
        out = out.reshape(chunk, columns, 2 * LANES)
        return out[:, :, :LANES], out[:, :, LANES:]

    def step(index, carry):
        first = pl.multiple_of(index * chunk, chunk)
        upper, lower = pl.ds(first, chunk), pl.ds(outer + first, chunk)
        cos_turn, sin_turn = cos_ref[upper], sin_ref[upper]
        real, imag = spread[upper], spread[lower]
        real, imag = times(
            real * cos_turn + imag * sin_turn, imag * cos_turn - real * sin_turn, forward
        )
        kernel_real, kernel_imag = real[:, 2 * wide :], imag[:, 2 * wide :]
        mixed_reals, mixed_imags, back_reals, back_imags = [], [], [], []
        corr_real, corr_imag = 0.0, 0.0
        for seq in range(seqs):
            near = slice(seq * share, (seq + 1) * share)
            far = slice(wide + seq * share, wide + (seq + 1) * share)
            value_real, value_imag = real[:, near], imag[:, near]
            grad_real, grad_imag = real[:, far], imag[:, far]
            mixed_reals.append(value_real * kernel_real - value_imag * kernel_imag)
            mixed_imags.append(value_real * kernel_imag + value_imag * kernel_real)
            back_reals.append(grad_real * kernel_real + grad_imag * kernel_imag)
            back_imags.append(grad_imag * kernel_real - grad_real * kernel_imag)
            corr_real = corr_real + grad_real * value_real + grad_imag * value_imag
            corr_imag = corr_imag + grad_imag * value_real - grad_real * value_imag
        real, imag = times(
            jnp.concatenate(mixed_reals + back_reals + [corr_real], axis=1),
            jnp.concatenate(mixed_imags + back_imags + [corr_imag], axis=1),
            inverse,
        )
        turned[upper] = real * cos_turn - imag * sin_turn
        turned[lower] = imag * cos_turn + real * sin_turn
        return carry

    lax.fori_loop(0, outer // chunk, step, 0)


def convolve_all(packed, seqs, share):
    outer, columns, _ = packed.shape
    length = outer * LANES
    wide = seqs * share
    tables = dft_tables(length)
    forward_first, inverse_first, forward_second, inverse_second, cos_turn, sin_turn = tables
    high, low = split_table(forward_first)
    flat = packed.reshape(outer, columns * LANES)
    spread = dot(jnp.concatenate([high, low], axis=1), jnp.concatenate([flat, flat], axis=0))
    spread = spread.reshape(2 * outer, columns, LANES)
    turned = pl.pallas_call(
        functools.partial(spectra_kernel, seqs, share),
        out_shape=jax.ShapeDtypeStruct(spread.shape, jnp.float32),
        in_specs=[pl.BlockSpec(memory_space=pltpu.VMEM)] * 5,
        out_specs=pl.BlockSpec(memory_space=pltpu.VMEM),
        compiler_params=pltpu.CompilerParams(vmem_limit_bytes=48 * 2**20),
        name="spectra",
    )(spread, cos_turn, sin_turn, stack_table(forward_second), stack_table(inverse_second))
    turned = turned.reshape(2 * outer, columns * LANES)
    rows = jnp.dot(inverse_first, turned, precision=lax.Precision.HIGH)
    return rows.reshape(outer, columns, LANES)


def local(inputs, value_weight, gate_weight, output_weight, filters, cotangent):
    token_rows = inputs[0]
    upstream = cotangent[0]
    tok_rows, width = token_rows.shape
    count = lax.axis_size("ctx")
    seqs = lax.axis_size("dp")
    peers = count * seqs
    share = width // peers
    tiles = tok_rows // LANES
    half = tok_rows // seqs
    value_act = contract(value_weight, 0, token_rows, 1).astype(jnp.bfloat16)
    gate_act = contract(gate_weight, 0, token_rows, 1)
    d_gated = contract(output_weight, 1, upstream, 1)
    d_mixed = (d_gated * gate_act).astype(jnp.bfloat16)
    kernel_part = lax.dynamic_slice_in_dim(filters, lax.axis_index("dp") * half, half, 0).T
    sent = jnp.concatenate(
        [
            value_act.reshape(peers, share * tiles, LANES),
            d_mixed.reshape(peers, share * tiles, LANES),
            kernel_part.reshape(peers, share * half // LANES, LANES),
        ],
        axis=1,
    )
    held = exchange(sent, 0)
    cut = share * tiles
    fields = held[:, : 2 * cut].reshape(count, seqs, 2, share, tiles, LANES)
    fields = fields.transpose(0, 4, 2, 1, 3, 5).reshape(count * tiles, 2 * seqs * share, LANES)
    taps = held[:, 2 * cut :].reshape(count, seqs, share, half // LANES, LANES)
    taps = taps.transpose(0, 1, 3, 2, 4).reshape(count * tiles, share, LANES)
    rows = convolve_all(jnp.concatenate([fields, taps], axis=1), seqs, share)
    grad_scale = 1.0 / math.sqrt(seqs * count * tok_rows)
    wide = seqs * share
    fields = rows[:, : 2 * wide].astype(jnp.bfloat16)
    fields = fields.reshape(count, tiles, 2, seqs, share, LANES).transpose(0, 3, 2, 4, 1, 5)
    terms = (rows[:, 2 * wide :] * grad_scale).astype(jnp.bfloat16)
    near = tiles // seqs
    terms = terms.reshape(count, seqs, near, share, LANES).transpose(0, 1, 3, 2, 4)
    back = exchange(
        jnp.concatenate(
            [
                fields.reshape(peers, 2 * share * tiles, LANES),
                terms.reshape(peers, share * near, LANES),
            ],
            axis=1,
        ),
        1,
    )
    mixed_act = back[:, :cut].reshape(width, tok_rows).astype(jnp.float32)
    d_value = back[:, cut : 2 * cut].reshape(width, tok_rows)
    gated = (gate_act * mixed_act).astype(jnp.bfloat16)
    d_gate = (d_gated * mixed_act).astype(jnp.bfloat16)
    input_rows = contract(d_value, 0, value_weight, 1) + contract(d_gate, 0, gate_weight, 1)
    input_grad = input_rows.astype(jnp.bfloat16)[None]
    proj_terms = jnp.stack(
        [
            contract(token_rows, 0, d_value, 1),
            contract(token_rows, 0, d_gate, 1),
            dot(gated, upstream),
        ],
        axis=0,
    )
    proj_terms = (proj_terms * grad_scale).astype(jnp.bfloat16)
    cell = width // count
    part = cell // seqs
    pack = width // LANES
    proj_terms = proj_terms.reshape(3, count, seqs, part, width).transpose(2, 1, 0, 3, 4)
    proj_sums, all_terms = reduce_and_join(
        proj_terms.reshape(seqs, count, 3 * part * pack, LANES),
        back[:, 2 * cut :].reshape(width * near, LANES),
        2,
    )
    proj_grads = proj_sums.reshape(seqs, 3, part, width).transpose(1, 0, 2, 3)
    proj_grads = proj_grads.reshape(3, cell, width)
    filter_grads = all_terms.reshape(seqs, width, half).transpose(0, 2, 1)
    filter_grads = filter_grads.reshape(tok_rows, width).astype(jnp.float32)
    return (input_grad, proj_grads, filter_grads)


def solution(mesh):
    return jax.shard_map(
        local,
        mesh=mesh,
        in_specs=(
            P(("groups", "dp"), "ctx", None),
            P(),
            P(),
            P(),
            P("ctx", None),
            P(("groups", "dp"), "ctx", None),
        ),
        out_specs=(
            P(("groups", "dp"), "ctx", None),
            P("groups", "ctx", None),
            P(("groups", "ctx"), None),
        ),
        check_vma=False,
    )
```

```python
import functools
import math

import jax
import jax.numpy as jnp
import numpy as np
from jax import lax
from jax.experimental import pallas as pl
from jax.experimental.pallas import tpu as pltpu
from jax.sharding import PartitionSpec as P

LANES = 128
AXES = ("ctx", "dp")


def dft_tables(length):
    outer = length // LANES
    k_outer = np.arange(outer)
    k_inner = np.arange(LANES)
    first = 2.0 * np.pi / outer * (np.outer(k_outer, k_outer) % outer)
    turn = 2.0 * np.pi / length * (np.outer(k_outer, k_inner) % length)
    second = 2.0 * np.pi / LANES * (np.outer(k_inner, k_inner) % LANES)
    cos_first, sin_first = np.cos(first), np.sin(first)
    cos_second, sin_second = np.cos(second), np.sin(second)
    forward_first = np.concatenate([cos_first, -sin_first], axis=0)
    inverse_first = np.concatenate([cos_first, -sin_first], axis=1) / length
    forward_second = np.block([[cos_second, -sin_second], [sin_second, cos_second]])
    inverse_second = np.block([[cos_second, sin_second], [-sin_second, cos_second]])
    as_float = [
        table.astype(np.float32)
        for table in (forward_first, inverse_first, forward_second, inverse_second)
    ]
    cos_turn = np.cos(turn).astype(np.float32)[:, None, :]
    sin_turn = np.sin(turn).astype(np.float32)[:, None, :]
    return as_float + [cos_turn, sin_turn]


def split(value):
    high = value.astype(jnp.bfloat16)
    low = (value - high.astype(jnp.float32)).astype(jnp.bfloat16)
    return high, low


def split_table(table):
    high = table.astype(jnp.bfloat16)
    return high, (table - high.astype(np.float32)).astype(jnp.bfloat16)


def dot(left, right):
    return jnp.dot(left, right, preferred_element_type=jnp.float32)


def contract(left, left_dim, right, right_dim):
    return lax.dot_general(
        left, right, (((left_dim,), (right_dim,)), ((), ())), preferred_element_type=jnp.float32
    )


def exchange_kernel(count, seqs, sent, held, send_sem, recv_sem, own_sem):
    peers = count * seqs
    me = lax.axis_index("ctx") * seqs + lax.axis_index("dp")
    barrier = pltpu.get_barrier_semaphore()

    def place(step):
        peer = lax.rem(me + step, peers)
        return peer, {"ctx": lax.div(peer, seqs), "dp": lax.rem(peer, seqs)}

    def greet(step, carry):
        pl.semaphore_signal(
            barrier, inc=1, device_id=place(step)[1], device_id_type=pl.DeviceIdType.MESH
        )
        return carry

    lax.fori_loop(1, peers, greet, 0)
    own = pltpu.make_async_copy(sent.at[me], held.at[me], own_sem)
    own.start()
    pl.semaphore_wait(barrier, peers - 1)

    def remote(step):
        peer, target = place(step)
        return pltpu.make_async_remote_copy(
            src_ref=sent.at[peer],
            dst_ref=held.at[me],
            send_sem=send_sem.at[step],
            recv_sem=recv_sem.at[step],
            device_id=target,
            device_id_type=pl.DeviceIdType.MESH,
        )

    def launch(turn, carry):
        away = lax.div(turn + 1, 2) * (1 - 2 * lax.rem(turn, 2))
        remote(peers // 2 + away).start()
        return carry

    def finish(step, carry):
        remote(step).wait()
        return carry

    lax.fori_loop(0, peers - 1, launch, 0)
    own.wait()
    lax.fori_loop(1, peers, finish, 0)


def exchange(blocks, collective_id):
    count, seqs = lax.axis_size("ctx"), lax.axis_size("dp")
    peers, rows, lanes = blocks.shape
    extra = -rows % 16
    if extra:
        blocks = jnp.pad(blocks, ((0, 0), (0, extra), (0, 0)))
    held = pl.pallas_call(
        functools.partial(exchange_kernel, count, seqs),
        out_shape=jax.ShapeDtypeStruct(blocks.shape, blocks.dtype),
        in_specs=[pl.BlockSpec(memory_space=pltpu.VMEM)],
        out_specs=pl.BlockSpec(memory_space=pltpu.VMEM),
        scratch_shapes=[
            pltpu.SemaphoreType.DMA((peers,)),
            pltpu.SemaphoreType.DMA((peers,)),
            pltpu.SemaphoreType.DMA,
        ],
        compiler_params=pltpu.CompilerParams(
            collective_id=collective_id, has_side_effects=True, vmem_limit_bytes=32 * 2**20
        ),
        name="exchange",
    )(blocks)
    return held[:, :rows] if extra else held


def reduce_kernel(count, proj, terms, sums, all_terms, other, stage, held, send_sem, recv_sem, go_sem, come_sem):
    place = lax.axis_index("ctx")
    core = lax.axis_index("dp")
    barrier = pltpu.get_barrier_semaphore()

    def send(source, target, slot):
        return pltpu.make_async_remote_copy(
            src_ref=source,
            dst_ref=target,
            send_sem=send_sem.at[slot],
            recv_sem=recv_sem.at[slot],
            device_id={"dp": 1 - core},
            device_id_type=pl.DeviceIdType.MESH,
        )

    def across(step):
        peer = lax.rem(place + step, count)
        return pltpu.make_async_remote_copy(
            src_ref=stage.at[peer],
            dst_ref=held.at[place],
            send_sem=go_sem.at[step],
            recv_sem=come_sem.at[step],
            device_id={"ctx": peer},
            device_id_type=pl.DeviceIdType.MESH,
        )

    def greet(step, carry):
        pl.semaphore_signal(
            barrier,
            inc=1,
            device_id={"ctx": lax.rem(place + step, count)},
            device_id_type=pl.DeviceIdType.MESH,
        )
        return carry

    def outwards(turn):
        return count // 2 + lax.div(turn + 1, 2) * (1 - 2 * lax.rem(turn, 2))

    def half(step):
        peer = lax.rem(place + step, count)
        return send(proj.at[1 - core, peer], other.at[peer], step)

    def offer(turn, carry):
        half(outwards(turn)).start()
        return carry

    def join(step):
        half(step).wait()
        peer = lax.rem(place + step, count)
        stage[peer] = (
            proj[core, peer].astype(jnp.float32) + other[peer].astype(jnp.float32)
        ).astype(jnp.bfloat16)

    def launch(turn, carry):
        step = outwards(turn)
        join(step)
        across(step).start()
        return carry

    def finish(step, carry):
        across(step).wait()
        return carry

    def add(step, total):
        return total + held[lax.rem(place + step, count)].astype(jnp.float32)

    pl.semaphore_signal(
        barrier, inc=1, device_id={"dp": 1 - core}, device_id_type=pl.DeviceIdType.MESH
    )
    lax.fori_loop(1, count, greet, 0)
    pl.semaphore_wait(barrier, count)
    lax.fori_loop(0, count, offer, 0)
    taps = send(terms, all_terms.at[core], count)
    taps.start()
    all_terms[core] = terms[...]
    lax.fori_loop(0, count - 1, launch, 0)
    join(0)
    taps.wait()
    lax.fori_loop(1, count, finish, 0)
    sums[core] = lax.fori_loop(1, count, add, stage[place].astype(jnp.float32))
    total = send(sums.at[core], sums.at[core], count + 1)
    total.start()
    total.wait()


def reduce_and_join(proj, terms, collective_id):
    count = lax.axis_size("ctx")
    rows = proj.shape[2]
    extra = -rows % 16
    if extra:
        proj = jnp.pad(proj, ((0, 0), (0, 0), (0, extra), (0, 0)))
    part = proj.shape[1:]
    sums, all_terms = pl.pallas_call(
        functools.partial(reduce_kernel, count),
        out_shape=(
            jax.ShapeDtypeStruct((2,) + part[1:], jnp.float32),
            jax.ShapeDtypeStruct((2,) + terms.shape, terms.dtype),
        ),
        in_specs=[pl.BlockSpec(memory_space=pltpu.VMEM)] * 2,
        out_specs=(pl.BlockSpec(memory_space=pltpu.VMEM),) * 2,
        scratch_shapes=[
            pltpu.VMEM(part, jnp.bfloat16),
            pltpu.VMEM(part, jnp.bfloat16),
            pltpu.VMEM(part, jnp.bfloat16),
            pltpu.SemaphoreType.DMA((count + 2,)),
            pltpu.SemaphoreType.DMA((count + 2,)),
            pltpu.SemaphoreType.DMA((count,)),
            pltpu.SemaphoreType.DMA((count,)),
        ],
        compiler_params=pltpu.CompilerParams(
            collective_id=collective_id, has_side_effects=True, vmem_limit_bytes=32 * 2**20
        ),
        name="reduce_and_join",
    )(proj, terms)
    return sums[:, :rows], all_terms


def stack_table(table):
    high, low = split_table(table)
    return jnp.concatenate([high, high, low], axis=0)


def spectra_kernel(seqs, share, spread, cos_ref, sin_ref, forward, inverse, turned):
    outer = spread.shape[0] // 2
    columns = spread.shape[1]
    wide = seqs * share
    chunk = 8

    def times(real, imag, table):
        both = jnp.concatenate([real, imag], axis=2).reshape(chunk * columns, 2 * LANES)
        high, low = split(both)
        out = dot(jnp.concatenate([high, low, high], axis=1), table[...])
        out = out.reshape(chunk, columns, 2 * LANES)
        return out[:, :, :LANES], out[:, :, LANES:]

    def step(index, carry):
        first = pl.multiple_of(index * chunk, chunk)
        upper, lower = pl.ds(first, chunk), pl.ds(outer + first, chunk)
        cos_turn, sin_turn = cos_ref[upper], sin_ref[upper]
        real, imag = spread[upper], spread[lower]
        real, imag = times(
            real * cos_turn + imag * sin_turn, imag * cos_turn - real * sin_turn, forward
        )
        kernel_real, kernel_imag = real[:, 2 * wide :], imag[:, 2 * wide :]
        mixed_reals, mixed_imags, back_reals, back_imags = [], [], [], []
        corr_real, corr_imag = 0.0, 0.0
        for seq in range(seqs):
            near = slice(seq * share, (seq + 1) * share)
            far = slice(wide + seq * share, wide + (seq + 1) * share)
            value_real, value_imag = real[:, near], imag[:, near]
            grad_real, grad_imag = real[:, far], imag[:, far]
            mixed_reals.append(value_real * kernel_real - value_imag * kernel_imag)
            mixed_imags.append(value_real * kernel_imag + value_imag * kernel_real)
            back_reals.append(grad_real * kernel_real + grad_imag * kernel_imag)
            back_imags.append(grad_imag * kernel_real - grad_real * kernel_imag)
            corr_real = corr_real + grad_real * value_real + grad_imag * value_imag
            corr_imag = corr_imag + grad_imag * value_real - grad_real * value_imag
        real, imag = times(
            jnp.concatenate(mixed_reals + back_reals + [corr_real], axis=1),
            jnp.concatenate(mixed_imags + back_imags + [corr_imag], axis=1),
            inverse,
        )
        turned[upper] = real * cos_turn - imag * sin_turn
        turned[lower] = imag * cos_turn + real * sin_turn
        return carry

    lax.fori_loop(0, outer // chunk, step, 0)


def convolve_all(packed, seqs, share):
    outer, columns, _ = packed.shape
    length = outer * LANES
    wide = seqs * share
    tables = dft_tables(length)
    forward_first, inverse_first, forward_second, inverse_second, cos_turn, sin_turn = tables
    high, low = split_table(forward_first)
    flat = packed.reshape(outer, columns * LANES)
    spread = dot(jnp.concatenate([high, low], axis=1), jnp.concatenate([flat, flat], axis=0))
    spread = spread.reshape(2 * outer, columns, LANES)
    turned = pl.pallas_call(
        functools.partial(spectra_kernel, seqs, share),
        out_shape=jax.ShapeDtypeStruct(spread.shape, jnp.float32),
        in_specs=[pl.BlockSpec(memory_space=pltpu.VMEM)] * 5,
        out_specs=pl.BlockSpec(memory_space=pltpu.VMEM),
        compiler_params=pltpu.CompilerParams(vmem_limit_bytes=48 * 2**20),
        name="spectra",
    )(spread, cos_turn, sin_turn, stack_table(forward_second), stack_table(inverse_second))
    turned = turned.reshape(2 * outer, columns * LANES)
    rows = jnp.dot(inverse_first, turned, precision=lax.Precision.HIGH)
    return rows.reshape(outer, columns, LANES)


def local(inputs, value_weight, gate_weight, output_weight, filters, cotangent):
    token_rows = inputs[0]
    upstream = cotangent[0]
    tok_rows, width = token_rows.shape
    count = lax.axis_size("ctx")
    seqs = lax.axis_size("dp")
    peers = count * seqs
    share = width // peers
    tiles = tok_rows // LANES
    half = tok_rows // seqs
    value_act = contract(value_weight, 0, token_rows, 1).astype(jnp.bfloat16)
    gate_act = contract(gate_weight, 0, token_rows, 1)
    d_gated = contract(output_weight, 1, upstream, 1)
    d_mixed = (d_gated * gate_act).astype(jnp.bfloat16)
    kernel_part = lax.dynamic_slice_in_dim(filters, lax.axis_index("dp") * half, half, 0).T
    sent = jnp.concatenate(
        [
            value_act.reshape(peers, share * tiles, LANES),
            d_mixed.reshape(peers, share * tiles, LANES),
            kernel_part.reshape(peers, share * half // LANES, LANES),
        ],
        axis=1,
    )
    held = exchange(sent, 0)
    cut = share * tiles
    fields = held[:, : 2 * cut].reshape(count, seqs, 2, share, tiles, LANES)
    fields = fields.transpose(0, 4, 2, 1, 3, 5).reshape(count * tiles, 2 * seqs * share, LANES)
    taps = held[:, 2 * cut :].reshape(count, seqs, share, half // LANES, LANES)
    taps = taps.transpose(0, 1, 3, 2, 4).reshape(count * tiles, share, LANES)
    rows = convolve_all(jnp.concatenate([fields, taps], axis=1), seqs, share)
    grad_scale = 1.0 / math.sqrt(seqs * count * tok_rows)
    wide = seqs * share
    fields = rows[:, : 2 * wide].astype(jnp.bfloat16)
    fields = fields.reshape(count, tiles, 2, seqs, share, LANES).transpose(0, 3, 2, 4, 1, 5)
    terms = (rows[:, 2 * wide :] * grad_scale).astype(jnp.bfloat16)
    near = tiles // seqs
    terms = terms.reshape(count, seqs, near, share, LANES).transpose(0, 1, 3, 2, 4)
    back = exchange(
        jnp.concatenate(
            [
                fields.reshape(peers, 2 * share * tiles, LANES),
                terms.reshape(peers, share * near, LANES),
            ],
            axis=1,
        ),
        1,
    )
    mixed_act = back[:, :cut].reshape(width, tok_rows).astype(jnp.float32)
    d_value = back[:, cut : 2 * cut].reshape(width, tok_rows)
    gated = (gate_act * mixed_act).astype(jnp.bfloat16)
    d_gate = (d_gated * mixed_act).astype(jnp.bfloat16)
    input_rows = contract(d_value, 0, value_weight, 1) + contract(d_gate, 0, gate_weight, 1)
    input_grad = input_rows.astype(jnp.bfloat16)[None]
    proj_terms = jnp.stack(
        [
            contract(token_rows, 0, d_value, 1),
            contract(token_rows, 0, d_gate, 1),
            dot(gated, upstream),
        ],
        axis=0,
    )
    proj_terms = (proj_terms * grad_scale).astype(jnp.bfloat16)
    cell = width // count
    part = cell // seqs
    pack = width // LANES
    proj_terms = proj_terms.reshape(3, count, seqs, part, width).transpose(2, 1, 0, 3, 4)
    proj_sums, all_terms = reduce_and_join(
        proj_terms.reshape(seqs, count, 3 * part * pack, LANES),
        back[:, 2 * cut :].reshape(width * near, LANES),
        2,
    )
    proj_grads = proj_sums.reshape(seqs, 3, part, width).transpose(1, 0, 2, 3)
    proj_grads = proj_grads.reshape(3, cell, width)
    filter_grads = all_terms.reshape(seqs, width, half).transpose(0, 2, 1)
    filter_grads = filter_grads.reshape(tok_rows, width).astype(jnp.float32)
    return (input_grad, proj_grads, filter_grads)


def solution(mesh):
    return jax.shard_map(
        local,
        mesh=mesh,
        in_specs=(
            P(("groups", "dp"), "ctx", None),
            P(),
            P(),
            P(),
            P("ctx", None),
            P(("groups", "dp"), "ctx", None),
        ),
        out_specs=(
            P(("groups", "dp"), "ctx", None),
            P("groups", "ctx", None),
            P(("groups", "ctx"), None),
        ),
        check_vma=False,
    )
```

```python
import functools
import math

import jax
import jax.numpy as jnp
import numpy as np
from jax import lax
from jax.experimental import pallas as pl
from jax.experimental.pallas import tpu as pltpu
from jax.sharding import PartitionSpec as P

LANES = 128
AXES = ("ctx", "dp")


def dft_tables(length):
    outer = length // LANES
    k_outer = np.arange(outer)
    k_inner = np.arange(LANES)
    first = 2.0 * np.pi / outer * (np.outer(k_outer, k_outer) % outer)
    turn = 2.0 * np.pi / length * (np.outer(k_outer, k_inner) % length)
    second = 2.0 * np.pi / LANES * (np.outer(k_inner, k_inner) % LANES)
    cos_first, sin_first = np.cos(first), np.sin(first)
    cos_second, sin_second = np.cos(second), np.sin(second)
    forward_first = np.concatenate([cos_first, -sin_first], axis=0)
    inverse_first = np.concatenate([cos_first, -sin_first], axis=1) / length
    forward_second = np.block([[cos_second, -sin_second], [sin_second, cos_second]])
    inverse_second = np.block([[cos_second, sin_second], [-sin_second, cos_second]])
    as_float = [
        table.astype(np.float32)
        for table in (forward_first, inverse_first, forward_second, inverse_second)
    ]
    cos_turn = np.cos(turn).astype(np.float32)[:, None, :]
    sin_turn = np.sin(turn).astype(np.float32)[:, None, :]
    return as_float + [cos_turn, sin_turn]


def split(value):
    high = value.astype(jnp.bfloat16)
    low = (value - high.astype(jnp.float32)).astype(jnp.bfloat16)
    return high, low


def split_table(table):
    high = table.astype(jnp.bfloat16)
    return high, (table - high.astype(np.float32)).astype(jnp.bfloat16)


def dot(left, right):
    return jnp.dot(left, right, preferred_element_type=jnp.float32)


def contract(left, left_dim, right, right_dim):
    return lax.dot_general(
        left, right, (((left_dim,), (right_dim,)), ((), ())), preferred_element_type=jnp.float32
    )


def exchange_kernel(count, seqs, sent, held, send_sem, recv_sem, own_sem):
    peers = count * seqs
    me = lax.axis_index("ctx") * seqs + lax.axis_index("dp")
    barrier = pltpu.get_barrier_semaphore()

    def place(step):
        peer = lax.rem(me + step, peers)
        return peer, {"ctx": lax.div(peer, seqs), "dp": lax.rem(peer, seqs)}

    def greet(step, carry):
        pl.semaphore_signal(
            barrier, inc=1, device_id=place(step)[1], device_id_type=pl.DeviceIdType.MESH
        )
        return carry

    lax.fori_loop(1, peers, greet, 0)
    own = pltpu.make_async_copy(sent.at[me], held.at[me], own_sem)
    own.start()
    pl.semaphore_wait(barrier, peers - 1)

    def remote(step):
        peer, target = place(step)
        return pltpu.make_async_remote_copy(
            src_ref=sent.at[peer],
            dst_ref=held.at[me],
            send_sem=send_sem.at[step],
            recv_sem=recv_sem.at[step],
            device_id=target,
            device_id_type=pl.DeviceIdType.MESH,
        )

    def launch(turn, carry):
        away = lax.div(turn + 1, 2) * (1 - 2 * lax.rem(turn, 2))
        remote(peers // 2 + away).start()
        return carry

    def finish(step, carry):
        remote(step).wait()
        return carry

    lax.fori_loop(0, peers - 1, launch, 0)
    own.wait()
    lax.fori_loop(1, peers, finish, 0)


def exchange(blocks, collective_id):
    count, seqs = lax.axis_size("ctx"), lax.axis_size("dp")
    peers, rows, lanes = blocks.shape
    extra = -rows % 16
    if extra:
        blocks = jnp.pad(blocks, ((0, 0), (0, extra), (0, 0)))
    held = pl.pallas_call(
        functools.partial(exchange_kernel, count, seqs),
        out_shape=jax.ShapeDtypeStruct(blocks.shape, blocks.dtype),
        in_specs=[pl.BlockSpec(memory_space=pltpu.VMEM)],
        out_specs=pl.BlockSpec(memory_space=pltpu.VMEM),
        scratch_shapes=[
            pltpu.SemaphoreType.DMA((peers,)),
            pltpu.SemaphoreType.DMA((peers,)),
            pltpu.SemaphoreType.DMA,
        ],
        compiler_params=pltpu.CompilerParams(
            collective_id=collective_id, has_side_effects=True, vmem_limit_bytes=32 * 2**20
        ),
        name="exchange",
    )(blocks)
    return held[:, :rows] if extra else held


def reduce_kernel(count, proj, terms, sums, all_terms, other, stage, held, send_sem, recv_sem, go_sem, come_sem):
    place = lax.axis_index("ctx")
    core = lax.axis_index("dp")
    barrier = pltpu.get_barrier_semaphore()

    def send(source, target, slot):
        return pltpu.make_async_remote_copy(
            src_ref=source,
            dst_ref=target,
            send_sem=send_sem.at[slot],
            recv_sem=recv_sem.at[slot],
            device_id={"dp": 1 - core},
            device_id_type=pl.DeviceIdType.MESH,
        )

    def across(step):
        peer = lax.rem(place + step, count)
        return pltpu.make_async_remote_copy(
            src_ref=stage.at[peer],
            dst_ref=held.at[place],
            send_sem=go_sem.at[step],
            recv_sem=come_sem.at[step],
            device_id={"ctx": peer},
            device_id_type=pl.DeviceIdType.MESH,
        )

    def greet(step, carry):
        pl.semaphore_signal(
            barrier,
            inc=1,
            device_id={"ctx": lax.rem(place + step, count)},
            device_id_type=pl.DeviceIdType.MESH,
        )
        return carry

    def launch(step, carry):
        across(step).start()
        return carry

    def finish(step, carry):
        across(step).wait()
        return carry

    def add(step, total):
        return total + held[lax.rem(place + step, count)].astype(jnp.float32)

    pl.semaphore_signal(
        barrier, inc=1, device_id={"dp": 1 - core}, device_id_type=pl.DeviceIdType.MESH
    )
    lax.fori_loop(1, count, greet, 0)
    pl.semaphore_wait(barrier, count)
    halves = send(proj.at[1 - core], other, 0)
    halves.start()
    taps = send(terms, all_terms.at[core], 1)
    taps.start()
    all_terms[core] = terms[...]
    halves.wait()
    stage[...] = (proj[core].astype(jnp.float32) + other[...].astype(jnp.float32)).astype(
        jnp.bfloat16
    )
    lax.fori_loop(1, count, launch, 0)
    taps.wait()
    lax.fori_loop(1, count, finish, 0)
    sums[core] = lax.fori_loop(1, count, add, stage[place].astype(jnp.float32))
    total = send(sums.at[core], sums.at[core], 2)
    total.start()
    total.wait()


def reduce_and_join(proj, terms, collective_id):
    count = lax.axis_size("ctx")
    rows = proj.shape[2]
    extra = -rows % 16
    if extra:
        proj = jnp.pad(proj, ((0, 0), (0, 0), (0, extra), (0, 0)))
    part = proj.shape[1:]
    sums, all_terms = pl.pallas_call(
        functools.partial(reduce_kernel, count),
        out_shape=(
            jax.ShapeDtypeStruct((2,) + part[1:], jnp.float32),
            jax.ShapeDtypeStruct((2,) + terms.shape, terms.dtype),
        ),
        in_specs=[pl.BlockSpec(memory_space=pltpu.VMEM)] * 2,
        out_specs=(pl.BlockSpec(memory_space=pltpu.VMEM),) * 2,
        scratch_shapes=[
            pltpu.VMEM(part, jnp.bfloat16),
            pltpu.VMEM(part, jnp.bfloat16),
            pltpu.VMEM(part, jnp.bfloat16),
            pltpu.SemaphoreType.DMA((3,)),
            pltpu.SemaphoreType.DMA((3,)),
            pltpu.SemaphoreType.DMA((count,)),
            pltpu.SemaphoreType.DMA((count,)),
        ],
        compiler_params=pltpu.CompilerParams(
            collective_id=collective_id, has_side_effects=True, vmem_limit_bytes=32 * 2**20
        ),
        name="reduce_and_join",
    )(proj, terms)
    return sums[:, :rows], all_terms


def stack_table(table):
    high, low = split_table(table)
    return jnp.concatenate([high, high, low], axis=0)


def spectra_kernel(seqs, share, spread, cos_ref, sin_ref, forward, inverse, turned):
    outer = spread.shape[0] // 2
    columns = spread.shape[1]
    wide = seqs * share
    chunk = 8

    def times(real, imag, table):
        both = jnp.concatenate([real, imag], axis=2).reshape(chunk * columns, 2 * LANES)
        high, low = split(both)
        out = dot(jnp.concatenate([high, low, high], axis=1), table[...])
        out = out.reshape(chunk, columns, 2 * LANES)
        return out[:, :, :LANES], out[:, :, LANES:]

    def step(index, carry):
        first = pl.multiple_of(index * chunk, chunk)
        upper, lower = pl.ds(first, chunk), pl.ds(outer + first, chunk)
        cos_turn, sin_turn = cos_ref[upper], sin_ref[upper]
        real, imag = spread[upper], spread[lower]
        real, imag = times(
            real * cos_turn + imag * sin_turn, imag * cos_turn - real * sin_turn, forward
        )
        kernel_real, kernel_imag = real[:, 2 * wide :], imag[:, 2 * wide :]
        mixed_reals, mixed_imags, back_reals, back_imags = [], [], [], []
        corr_real, corr_imag = 0.0, 0.0
        for seq in range(seqs):
            near = slice(seq * share, (seq + 1) * share)
            far = slice(wide + seq * share, wide + (seq + 1) * share)
            value_real, value_imag = real[:, near], imag[:, near]
            grad_real, grad_imag = real[:, far], imag[:, far]
            mixed_reals.append(value_real * kernel_real - value_imag * kernel_imag)
            mixed_imags.append(value_real * kernel_imag + value_imag * kernel_real)
            back_reals.append(grad_real * kernel_real + grad_imag * kernel_imag)
            back_imags.append(grad_imag * kernel_real - grad_real * kernel_imag)
            corr_real = corr_real + grad_real * value_real + grad_imag * value_imag
            corr_imag = corr_imag + grad_imag * value_real - grad_real * value_imag
        real, imag = times(
            jnp.concatenate(mixed_reals + back_reals + [corr_real], axis=1),
            jnp.concatenate(mixed_imags + back_imags + [corr_imag], axis=1),
            inverse,
        )
        turned[upper] = (real * cos_turn - imag * sin_turn).astype(jnp.bfloat16)
        turned[lower] = (imag * cos_turn + real * sin_turn).astype(jnp.bfloat16)
        return carry

    lax.fori_loop(0, outer // chunk, step, 0)


def convolve_all(packed, seqs, share):
    outer, columns, _ = packed.shape
    length = outer * LANES
    wide = seqs * share
    tables = dft_tables(length)
    forward_first, inverse_first, forward_second, inverse_second, cos_turn, sin_turn = tables
    high, low = split_table(forward_first)
    flat = packed.reshape(outer, columns * LANES)
    spread = dot(jnp.concatenate([high, low], axis=1), jnp.concatenate([flat, flat], axis=0))
    spread = spread.reshape(2 * outer, columns, LANES)
    turned = pl.pallas_call(
        functools.partial(spectra_kernel, seqs, share),
        out_shape=jax.ShapeDtypeStruct(spread.shape, jnp.bfloat16),
        in_specs=[pl.BlockSpec(memory_space=pltpu.VMEM)] * 5,
        out_specs=pl.BlockSpec(memory_space=pltpu.VMEM),
        compiler_params=pltpu.CompilerParams(vmem_limit_bytes=48 * 2**20),
        name="spectra",
    )(spread, cos_turn, sin_turn, stack_table(forward_second), stack_table(inverse_second))
    turned = turned.reshape(2 * outer, columns * LANES)
    high, low = split_table(inverse_first)
    rows = dot(jnp.concatenate([high, low], axis=1), jnp.concatenate([turned, turned], axis=0))
    return rows.reshape(outer, columns, LANES)


def local(inputs, value_weight, gate_weight, output_weight, filters, cotangent):
    token_rows = inputs[0]
    upstream = cotangent[0]
    tok_rows, width = token_rows.shape
    count = lax.axis_size("ctx")
    seqs = lax.axis_size("dp")
    peers = count * seqs
    share = width // peers
    tiles = tok_rows // LANES
    half = tok_rows // seqs
    value_act = contract(value_weight, 0, token_rows, 1).astype(jnp.bfloat16)
    gate_act = contract(gate_weight, 0, token_rows, 1)
    d_gated = contract(output_weight, 1, upstream, 1)
    d_mixed = (d_gated * gate_act).astype(jnp.bfloat16)
    kernel_part = lax.dynamic_slice_in_dim(filters, lax.axis_index("dp") * half, half, 0).T
    sent = jnp.concatenate(
        [
            value_act.reshape(peers, share * tiles, LANES),
            d_mixed.reshape(peers, share * tiles, LANES),
            kernel_part.reshape(peers, share * half // LANES, LANES),
        ],
        axis=1,
    )
    held = exchange(sent, 0)
    cut = share * tiles
    fields = held[:, : 2 * cut].reshape(count, seqs, 2, share, tiles, LANES)
    fields = fields.transpose(0, 4, 2, 1, 3, 5).reshape(count * tiles, 2 * seqs * share, LANES)
    taps = held[:, 2 * cut :].reshape(count, seqs, share, half // LANES, LANES)
    taps = taps.transpose(0, 1, 3, 2, 4).reshape(count * tiles, share, LANES)
    rows = convolve_all(jnp.concatenate([fields, taps], axis=1), seqs, share)
    grad_scale = 1.0 / math.sqrt(seqs * count * tok_rows)
    wide = seqs * share
    fields = rows[:, : 2 * wide].astype(jnp.bfloat16)
    fields = fields.reshape(count, tiles, 2, seqs, share, LANES).transpose(0, 3, 2, 4, 1, 5)
    terms = (rows[:, 2 * wide :] * grad_scale).astype(jnp.bfloat16)
    near = tiles // seqs
    terms = terms.reshape(count, seqs, near, share, LANES).transpose(0, 1, 3, 2, 4)
    back = exchange(
        jnp.concatenate(
            [
                fields.reshape(peers, 2 * share * tiles, LANES),
                terms.reshape(peers, share * near, LANES),
            ],
            axis=1,
        ),
        1,
    )
    mixed_act = back[:, :cut].reshape(width, tok_rows).astype(jnp.float32)
    d_value = back[:, cut : 2 * cut].reshape(width, tok_rows)
    gated = (gate_act * mixed_act).astype(jnp.bfloat16)
    d_gate = (d_gated * mixed_act).astype(jnp.bfloat16)
    input_rows = contract(d_value, 0, value_weight, 1) + contract(d_gate, 0, gate_weight, 1)
    input_grad = input_rows.astype(jnp.bfloat16)[None]
    proj_terms = jnp.stack(
        [
            contract(token_rows, 0, d_value, 1),
            contract(token_rows, 0, d_gate, 1),
            dot(gated, upstream),
        ],
        axis=0,
    )
    proj_terms = (proj_terms * grad_scale).astype(jnp.bfloat16)
    cell = width // count
    part = cell // seqs
    pack = width // LANES
    proj_terms = proj_terms.reshape(3, count, seqs, part, width).transpose(2, 1, 0, 3, 4)
    proj_sums, all_terms = reduce_and_join(
        proj_terms.reshape(seqs, count, 3 * part * pack, LANES),
        back[:, 2 * cut :].reshape(width * near, LANES),
        2,
    )
    proj_grads = proj_sums.reshape(seqs, 3, part, width).transpose(1, 0, 2, 3)
    proj_grads = proj_grads.reshape(3, cell, width)
    filter_grads = all_terms.reshape(seqs, width, half).transpose(0, 2, 1)
    filter_grads = filter_grads.reshape(tok_rows, width).astype(jnp.float32)
    return (input_grad, proj_grads, filter_grads)


def solution(mesh):
    return jax.shard_map(
        local,
        mesh=mesh,
        in_specs=(
            P(("groups", "dp"), "ctx", None),
            P(),
            P(),
            P(),
            P("ctx", None),
            P(("groups", "dp"), "ctx", None),
        ),
        out_specs=(
            P(("groups", "dp"), "ctx", None),
            P("groups", "ctx", None),
            P(("groups", "ctx"), None),
        ),
        check_vma=False,
    )
```
